256 devices in a mesh: seq: 64 (over z, y_lo, x), head: 4 (over y_hi, core).
Axes of the slice: x: 4, y: 4 (y_hi: 2, y_lo: 2; y = y_hi * 2 + y_lo), z: 8, core: 2. Of those that a mesh axis runs over, the one named last changes fastest.
Arguments:
- query: bfloat16 [32768, 4096], P('seq', 'head'), may hold values from -240 to 240
- keys: bfloat16 [64, 512, 1024], P('seq', None, 'head'), may hold values from -6 to 6
- values: bfloat16 [64, 512, 1024], P('seq', None, 'head'), may hold values from -6 to 6
- cotangent: bfloat16 [32768, 4096], P('seq', 'head'), may hold values from -6 to 6
- owner_map: int32 [64], replicated, may hold values from 0 to 63, as said below
- read_lists: int32 [256, 2], P('seq'), may hold values from 0 to 63, as said below
- visible: int32 [256, 2], P('seq'), may hold values from 0 to 1, as said below
Outputs:
- attended: bfloat16 [32768, 4096], P('seq', 'head')
- query_grad: bfloat16 [32768, 4096], P(('seq', 'head'))
- key_grad: bfloat16 [64, 512, 1024], P('seq', None, 'head')
- value_grad: bfloat16 [64, 512, 1024], P('seq', None, 'head')
The draws below stay inside these ranges and needn't reach their ends.
Inputs may be any that keep to these rules, and one draw needn't show every extreme that they name: A permutation: image i is held by the device at index owner_map[i] along seq. `read_lists`: every image listed for a text block of the device at index d along seq is held by the device at index d, d - 1 or d - 2; where both entries of a block are visible they name different images. The last text block of every device with d >= 2 lists the images held at d - 1 and d - 2, in that order. `visible`: on the last text block of every device, an entry is 1 wherever its image is held at a lower index than the reader.
All inputs are finite; a program needn't handle non-finite values.
Results may differ from the reference program's by a relative error of at most 0.028.
Values may be sent and summed in bfloat16 or wider, within the bound.
A program may use at most 64 MiB of HBM per device.

```python
import math
import jax
import jax.numpy as jnp
from jax import lax

HEADS = 32
KV_HEADS = 8
HD = 128
IMG_TOK = 512
BLOCK = 128
TOK_DEV = 512
IMAGES = 64
TOKENS = 32768
BLOCKS = 256
N_SEQ = 64


def layout(key):
    key_owner, key_pick, key_other, key_seen = jax.random.split(key, 4)
    owner = jax.random.permutation(key_owner, IMAGES).astype(jnp.int32)
    image_at = jnp.argsort(owner, stable=True).astype(jnp.int32)
    per_device = TOK_DEV // BLOCK
    block_ids = jnp.arange(BLOCKS, dtype=jnp.int32)
    device = block_ids // per_device
    final_block = block_ids % per_device == per_device - 1
    pick_one = jax.random.randint(key_pick, (BLOCKS,), 0, 3)
    pick_two = (pick_one + jax.random.randint(key_other, (BLOCKS,), 1, 3)) % 3
    pick_one = jnp.where(final_block, 1, pick_one)
    pick_two = jnp.where(final_block, 2, pick_two)
    distance = jnp.stack([pick_one, pick_two], axis=1).astype(jnp.int32)
    inside = distance <= device[:, None]
    holder = jnp.where(inside, device[:, None] - distance, device[:, None])
    listed = image_at[holder].astype(jnp.int32)
    random_seen = jax.random.randint(key_seen, (BLOCKS, 2), 0, 4) > 0
    seen = jnp.where(final_block[:, None], True, random_seen) & inside
    return (owner, listed, seen.astype(jnp.int32))


def draw_owner_map(key, part):
    return layout(key)[0]


def draw_read_lists(key, part):
    return layout(key)[1]


def draw_visible(key, part):
    return layout(key)[2]


def draw_query(key, part):
    key = jax.random.fold_in(key, 7)
    base = jnp.clip(jax.random.normal(key, (TOKENS, HEADS * HD), jnp.float32), -6.0, 6.0)
    return base.astype(jnp.bfloat16)


def block_levels(stream_key, dims, pieces, smallest, largest):
    def one(dim, blocks):
        steps = jax.random.uniform(jax.random.fold_in(jax.random.fold_in(stream_key, 6), dim), (blocks,), jnp.float32, smallest / len(pieces), largest / len(pieces))
        return jnp.repeat(jnp.exp(steps), dims[dim] // blocks).reshape((-1,) + (1,) * (len(dims) - dim - 1))

    loudness = one(*pieces[0])
    for cut in pieces[1:]:
        loudness = loudness * one(*cut)
    return loudness


def normal_values(own_key, shape, scale, reach, pieces=(), kind=jnp.bfloat16):
    result = scale * jax.random.normal(own_key, shape, jnp.float32)
    if pieces:
        result = result * block_levels(own_key, shape, pieces, -0.22, 0.18)
    return jnp.clip(result, -reach, reach).astype(kind)


def setup_inputs(seed: int = 0) -> dict:
    streams_of = jax.random.split(jax.random.key(seed), 8)
    return {
        "query": draw_query(jax.random.fold_in(streams_of[7], 71), 0),
        "keys": normal_values(streams_of[1], (IMAGES, IMG_TOK, KV_HEADS * HD), 1.0, 6.0, ((0, 64), (2, 4))),
        "values": normal_values(streams_of[2], (IMAGES, IMG_TOK, KV_HEADS * HD), 1.0, 6.0, ((0, 64), (2, 4))),
        "cotangent": normal_values(streams_of[3], (TOKENS, HEADS * HD), 1.0, 6.0, ((0, 64), (1, 4))),
        "owner_map": draw_owner_map(jax.random.fold_in(streams_of[7], 71), 0),
        "read_lists": draw_read_lists(jax.random.fold_in(streams_of[7], 71), 0),
        "visible": draw_visible(jax.random.fold_in(streams_of[7], 71), 0),
    }


def attend(query_block, key_block, value_block, grad_block, key_seen, scaling):
    query_f = query_block.astype(jnp.float32)
    key_f = key_block.astype(jnp.float32)
    value_f = value_block.astype(jnp.float32)
    grad_f = grad_block.astype(jnp.float32)
    score = jnp.einsum('rgqd,kgd->gqrk', query_f, key_f) * scaling
    live = key_seen[None, None, None, :]
    any_live = jnp.any(key_seen)
    row_max = lax.optimization_barrier(jnp.max(jnp.where(live, score, -1e+30), axis=3, keepdims=True))
    row_max = jnp.where(any_live, row_max, 0.0)
    weights = jnp.where(live, jnp.exp(score - row_max), 0.0)
    summed = lax.optimization_barrier(jnp.sum(weights, axis=3, keepdims=True))
    softmax = weights / jnp.where(any_live, summed, 1.0)
    weights_b = softmax.astype(jnp.bfloat16)
    attended = jnp.einsum('gqrk,kgd->rgqd', weights_b.astype(jnp.float32), value_f).astype(jnp.bfloat16)
    dprob = jnp.einsum('rgqd,kgd->gqrk', grad_f, value_f)
    row_dot = jnp.transpose(lax.optimization_barrier(jnp.sum(grad_f * attended.astype(jnp.float32), axis=3)), (1, 2, 0))[:, :, :, None]
    dscore = (softmax * (dprob - row_dot)).astype(jnp.bfloat16).astype(jnp.float32)
    query_grad = (jnp.einsum('gqrk,kgd->rgqd', dscore, key_f) * scaling).astype(jnp.bfloat16)
    key_grad = jnp.einsum('gqrk,rgqd->kgd', dscore, query_f) * scaling
    value_grad = jnp.einsum('gqrk,rgqd->kgd', weights_b.astype(jnp.float32), grad_f)
    return (attended, query_grad, key_grad, value_grad)

def reference(query, keys, values, cotangent, owner_map, read_lists, visible):
    scaling = 1.0 / math.sqrt(HD)
    per_device = TOK_DEV // BLOCK
    group = HEADS // KV_HEADS
    kv_columns = KV_HEADS * HD
    holders = owner_map[read_lists]
    query_split = query.reshape(N_SEQ, per_device, BLOCK, KV_HEADS, group, HD)
    grad_split = cotangent.reshape(N_SEQ, per_device, BLOCK, KV_HEADS, group, HD)
    holder_split = holders.reshape(N_SEQ, per_device, 2)
    seen_split = visible.reshape(N_SEQ, per_device, 2)
    pairs = jnp.stack([keys, values], axis=1)

    def device_step(accumulated, device_inputs):
        reader, query_dev, grad_dev, holder_dev, seen_dev = device_inputs
        distance = reader - holder_dev

        def block_step(partials, block_inputs):
            query_block, grad_block, holder_block, seen_block, dist_block = block_inputs
            gathered = pairs[holder_block]
            key_block = gathered[:, 0].reshape(2 * IMG_TOK, KV_HEADS, HD)
            value_block = gathered[:, 1].reshape(2 * IMG_TOK, KV_HEADS, HD)
            key_seen = jnp.repeat(seen_block > 0, IMG_TOK)
            attended, query_grad, key_grad, value_grad = attend(query_block, key_block, value_block, grad_block, key_seen, scaling)
            grads = jnp.stack([key_grad.reshape(2, IMG_TOK, kv_columns), value_grad.reshape(2, IMG_TOK, kv_columns)], axis=1)
            partials = partials.at[dist_block[0]].add(grads[0]).at[dist_block[1]].add(grads[1])
            return (partials, (attended, query_grad))
        zeros_start = jnp.zeros((3, 2, IMG_TOK, kv_columns), jnp.float32)
        partials, (attended, query_grad) = lax.scan(block_step, zeros_start, (query_dev, grad_dev, holder_dev, seen_dev, distance))
        rounded = lax.optimization_barrier(partials.astype(jnp.bfloat16)).astype(jnp.float32)
        for hop_index in range(3):
            holder_raw = reader - hop_index
            inside = holder_raw >= 0
            holder_at = jnp.maximum(holder_raw, 0)
            accumulated = accumulated.at[holder_at].add(jnp.where(inside, rounded[hop_index], jnp.float32(0.0)))
        return (accumulated, (attended, query_grad))
    start_sums = jnp.zeros((IMAGES, 2, IMG_TOK, kv_columns), jnp.float32)
    readers = jnp.arange(N_SEQ, dtype=jnp.int32)
    accumulated, (attended, query_grad) = lax.scan(device_step, start_sums, (readers, query_split, grad_split, holder_split, seen_split))
    attended = attended.reshape(TOKENS, HEADS * HD)
    query_grad = query_grad.reshape(TOKENS, HEADS * HD)
    return (attended, query_grad, accumulated[:, 0].astype(jnp.bfloat16), accumulated[:, 1].astype(jnp.bfloat16))
```

```python
import functools
import math

import jax
import jax.numpy as jnp
from jax import lax
from jax.experimental import pallas as pl
from jax.experimental.pallas import tpu as pltpu
from jax.sharding import PartitionSpec as P

HD = 128
BLOCK = 128
MESH = pl.DeviceIdType.MESH
F32, BF16 = jnp.float32, jnp.bfloat16
SCALE = 1.0 / math.sqrt(HD)
TO_EXP2 = SCALE * math.log2(math.e)
FAR = 1e30


def dot(a, b, ca, cb):
    return lax.dot_general(a, b, (((ca,), (cb,)), ((), ())), preferred_element_type=F32)


def kernel(
    sizes,
    query, keys, values, cotangent, owner_map, read_lists, visible,
    attended, query_rows, key_grad, value_grad,
    q_in, g_in, cand, att, dq_out, parts, send2, send1, got2, got1, own, result,
    load_sem, store_sem, fwd_send, fwd_recv, bwd_send, bwd_recv, dq_send, dq_recv, dq_own,
):
    n_seq, n_head, kv, group, blocks, img = sizes
    me = lax.axis_index("seq")
    head = lax.axis_index("head")
    after = lax.rem(me + 1, n_seq)
    before = lax.rem(me + n_seq - 1, n_seq)
    width = group * HD

    def cols(g):
        return pl.ds(g * HD, HD)

    loads = []
    for g in range(kv):
        loads.append(pltpu.make_async_copy(keys.at[0, :, cols(g)], cand[g].at[0, 0], load_sem.at[2 * g]))
        loads.append(pltpu.make_async_copy(values.at[0, :, cols(g)], cand[g].at[0, 1], load_sem.at[2 * g + 1]))
    loads.append(pltpu.make_async_copy(query, q_in, load_sem.at[2 * kv]))
    loads.append(pltpu.make_async_copy(cotangent, g_in, load_sem.at[2 * kv + 1]))
    for load in loads:
        load.start()

    barrier = pltpu.get_barrier_semaphore()
    for index in (before, after):
        pl.semaphore_signal(barrier, inc=1, device_id={"seq": index}, device_id_type=MESH)
    for step in range(1, n_head):
        pl.semaphore_signal(
            barrier, inc=1, device_id={"head": lax.rem(head + step, n_head)}, device_id_type=MESH
        )
    pl.semaphore_wait(barrier, n_head + 1)

    def to_next(g, hop, part):
        slot = 4 * g + 2 * hop + part
        return pltpu.make_async_remote_copy(
            cand[g].at[hop, part], cand[g].at[hop + 1, part], fwd_send.at[slot], fwd_recv.at[slot],
            device_id={"seq": after}, device_id_type=MESH,
        )

    def back(g, hop, part):
        slot = 4 * g + 2 * hop + part
        source, target = (send2, got2) if hop == 0 else (send1, got1)
        return pltpu.make_async_remote_copy(
            source.at[g, part], target.at[g, part], bwd_send.at[slot], bwd_recv.at[slot],
            device_id={"seq": before}, device_id_type=MESH,
        )

    def dq_copy(g, step, target):
        return pltpu.make_async_remote_copy(
            dq_out.at[g, step],
            query_rows.at[:, pl.ds(pl.multiple_of(head * kv * width + g * width, HD), width)],
            dq_send.at[g, step], dq_recv.at[g, step],
            device_id={"head": target}, device_id_type=MESH,
        )

    def dq_keep(g):
        return pltpu.make_async_copy(
            dq_out.at[g, blocks - 1],
            query_rows.at[:, pl.ds(pl.multiple_of(head * kv * width + g * width, HD), width)],
            dq_own.at[g],
        )

    def relay(g):
        for part in range(2):
            to_next(g, 0, part).wait_recv()
            to_next(g, 1, part).start()

    def add_on(g):
        for part in range(2):
            back(g, 0, part).wait_recv()
            send1[g, part] = (send1[g, part].astype(F32) + got2[g, part].astype(F32)).astype(BF16)
            back(g, 1, part).start()

    for load in loads[: 2 * kv]:
        load.wait()
    for part in range(2):
        to_next(0, 0, part).start()
    parts[:, 2] = jnp.zeros((blocks, 2, img, HD), F32)
    for load in loads[2 * kv :]:
        load.wait()
    relay(0)
    for g in range(1, kv):
        for part in range(2):
            to_next(g, 0, part).start()

    def distance(j, b):
        return jnp.clip(me - owner_map[read_lists[j, b]], 0, 2)

    away = [[distance(j, b) for j in range(2)] for b in range(blocks)]

    for g in range(kv):
        for part in range(2):
            to_next(g, 1, part).wait_recv()

        def block_step(step, carry, g=g):
            b = lax.rem(head + 1 + step, blocks)
            rows = pl.ds(pl.multiple_of(b * BLOCK, BLOCK), BLOCK)
            first, second = distance(0, b), distance(1, b)
            live0, live1 = visible[0, b] > 0, visible[1, b] > 0
            k0, k1 = cand[g][first, 0], cand[g][second, 0]
            v0, v1 = cand[g][first, 1], cand[g][second, 1]
            at_columns = [pl.ds((g * group + h) * HD, HD) for h in range(group)]
            qc = jnp.concatenate([q_in[rows, c] for c in at_columns], axis=0)
            gc = jnp.concatenate([g_in[rows, c] for c in at_columns], axis=0)
            s0, s1 = dot(k0, qc, 1, 1), dot(k1, qc, 1, 1)
            m0 = jnp.max(s0, axis=0, keepdims=True)
            m1 = jnp.max(s1, axis=0, keepdims=True)
            m = jnp.maximum(jnp.where(live0, m0, -FAR), jnp.where(live1, m1, -FAR)) * TO_EXP2
            e0 = jnp.exp2(s0 * TO_EXP2 - jnp.where(live0, m, FAR))
            e1 = jnp.exp2(s1 * TO_EXP2 - jnp.where(live1, m, FAR))
            total = jnp.sum(e0, axis=0, keepdims=True) + jnp.sum(e1, axis=0, keepdims=True)
            inverse = jnp.where(live0 | live1, 1.0 / jnp.where(live0 | live1, total, 1.0), 0.0)
            p0, p1 = e0 * inverse, e1 * inverse
            w0, w1 = p0.astype(BF16), p1.astype(BF16)
            d0, d1 = dot(v0, gc, 1, 1), dot(v1, gc, 1, 1)
            out = dot(v0, w0, 0, 0) + dot(v1, w1, 0, 0)
            row_dot = jnp.sum(p0 * d0, axis=0, keepdims=True) + jnp.sum(p1 * d1, axis=0, keepdims=True)
            c0 = (p0 * (d0 - row_dot)).astype(BF16)
            c1 = (p1 * (d1 - row_dot)).astype(BF16)
            dq = (dot(k0, c0, 0, 0) + dot(k1, c1, 0, 0)) * SCALE
            for h in range(group):
                part = slice(h * HD, (h + 1) * HD)
                att[rows, at_columns[h]] = out[:, part].T.astype(BF16)
                dq_out[g, step, :, h * HD : (h + 1) * HD] = dq[:, part].T.astype(BF16)
            parts[b, 0, 0] = dot(c0, qc, 1, 0) * SCALE
            parts[b, 0, 1] = dot(w0, gc, 1, 0)
            parts[b, 1, 0] = dot(c1, qc, 1, 0) * SCALE
            parts[b, 1, 1] = dot(w1, gc, 1, 0)

            @pl.when(step < blocks - 1)
            def _():
                dq_copy(g, step, b).start()

            @pl.when(step == blocks - 1)
            def _():
                dq_keep(g).start()

            @pl.when(step == 1)
            def _():
                if g + 1 < kv:
                    relay(g + 1)
                if g > 0:
                    add_on(g - 1)

            return carry

        lax.fori_loop(0, blocks, block_step, 0)

        def part_sum(slot, part):
            total = None
            for b in range(blocks):
                pick = jnp.where(away[b][0] == slot, 0, jnp.where(away[b][1] == slot, 1, 2))
                pick = jnp.where((away[b][0] == slot) & (away[b][1] == slot) & (visible[1, b] > 0), 1, pick)
                term = parts[b, pick, part]
                total = term if total is None else total + term
            return total

        for part in range(2):
            send2[g, part] = part_sum(2, part).astype(BF16)
            back(g, 0, part).start()
        for part in range(2):
            send1[g, part] = part_sum(1, part).astype(BF16)
        for part in range(2):
            own[g, part] = part_sum(0, part)

    stores = [pltpu.make_async_copy(att, attended, store_sem.at[0])]
    stores[0].start()
    add_on(kv - 1)
    for g in range(kv):
        for part, target in ((0, key_grad), (1, value_grad)):
            back(g, 1, part).wait_recv()
            result[g, part] = (own[g, part] + got1[g, part].astype(F32)).astype(BF16)
            store = pltpu.make_async_copy(
                result.at[g, part], target.at[0, :, cols(g)], store_sem.at[1 + 2 * g + part]
            )
            store.start()
            stores.append(store)
    for g in range(kv):
        for step in range(blocks - 1):
            copy = dq_copy(g, step, head)
            copy.wait_send()
            copy.wait_recv()
        dq_keep(g).wait()
        for hop in range(2):
            for part in range(2):
                to_next(g, hop, part).wait_send()
                back(g, hop, part).wait_send()
    for store in stores:
        store.wait()


def body(query, keys, values, cotangent, owner_map, read_lists, visible):
    rows, columns = query.shape
    img, kv_columns = keys.shape[1:]
    n_seq, n_head = lax.axis_size("seq"), lax.axis_size("head")
    kv = kv_columns // HD
    group = columns // kv_columns
    blocks = rows // BLOCK
    width = group * HD
    sizes = (n_seq, n_head, kv, group, blocks, img)
    any_space = pl.BlockSpec(memory_space=pl.ANY)
    scalar = pl.BlockSpec(memory_space=pltpu.SMEM)
    dma = pltpu.SemaphoreType.DMA
    return pl.pallas_call(
        functools.partial(kernel, sizes),
        out_shape=(
            jax.ShapeDtypeStruct((rows, columns), BF16),
            jax.ShapeDtypeStruct((rows // n_head, columns * n_head), BF16),
            jax.ShapeDtypeStruct(keys.shape, BF16),
            jax.ShapeDtypeStruct(values.shape, BF16),
        ),
        in_specs=[any_space] * 4 + [scalar] * 3,
        out_specs=(any_space,) * 4,
        scratch_shapes=[
            pltpu.VMEM((rows, columns), BF16),
            pltpu.VMEM((rows, columns), BF16),
            tuple(pltpu.VMEM((3, 2, img, HD), BF16) for _ in range(kv)),
            pltpu.VMEM((rows, columns), BF16),
            pltpu.VMEM((kv, blocks, BLOCK, width), BF16),
            pltpu.VMEM((blocks, 3, 2, img, HD), F32),
            pltpu.VMEM((kv, 2, img, HD), BF16),
            pltpu.VMEM((kv, 2, img, HD), BF16),
            pltpu.VMEM((kv, 2, img, HD), BF16),
            pltpu.VMEM((kv, 2, img, HD), BF16),
            pltpu.VMEM((kv, 2, img, HD), F32),
            pltpu.VMEM((kv, 2, img, HD), BF16),
            dma((2 * kv + 2,)),
            dma((1 + 2 * kv,)),
            dma((4 * kv,)),
            dma((4 * kv,)),
            dma((4 * kv,)),
            dma((4 * kv,)),
            dma((kv, blocks)),
            dma((kv, blocks)),
            dma((kv,)),
        ],
        compiler_params=pltpu.CompilerParams(
            collective_id=0, has_side_effects=True, vmem_limit_bytes=56 * 2**20
        ),
        name="cross_attention",
    )(query, keys, values, cotangent, owner_map, read_lists.T, visible.T)


def solution(mesh):
    in_specs = (
        P("seq", "head"),
        P("seq", None, "head"),
        P("seq", None, "head"),
        P("seq", "head"),
        P(),
        P("seq", None),
        P("seq", None),
    )
    out_specs = (
        P("seq", "head"),
        P(("seq", "head"), None),
        P("seq", None, "head"),
        P("seq", None, "head"),
    )
    return jax.shard_map(body, mesh=mesh, in_specs=in_specs, out_specs=out_specs, check_vma=False)
```

```python
import functools
import math

import jax
import jax.numpy as jnp
from jax import lax
from jax.experimental import pallas as pl
from jax.experimental.pallas import tpu as pltpu
from jax.sharding import PartitionSpec as P

HD = 128
BLOCK = 128
MESH = pl.DeviceIdType.MESH
F32, BF16 = jnp.float32, jnp.bfloat16
SCALE = 1.0 / math.sqrt(HD)
TO_EXP2 = SCALE * math.log2(math.e)
FAR = 1e30
CUT = 176
PIECES = 4


def dot(a, b, ca, cb):
    return lax.dot_general(a, b, (((ca,), (cb,)), ((), ())), preferred_element_type=F32)


def kernel(
    sizes,
    query, keys, values, cotangent, owner_map, read_lists, visible,
    attended, query_rows, key_grad, value_grad,
    q_in, g_in, cand, via_f, att, dq_out, soft, parts,
    out2a, out2b, out1a, out1b, got2a, got1a, got1b, via_b, far1b, own, result,
    load_sem, store_sem, fwd_send, fwd_recv, bwd_send, bwd_recv, dq_send, dq_recv, dq_own,
):
    n_seq, n_head, kv, group, blocks, img = sizes
    me = lax.axis_index("seq")
    head = lax.axis_index("head")
    width = group * HD

    last_seq = n_seq - 1
    after, before = me + 1, me - 1
    has_after, has_before = me < last_seq, me > 0
    has_after2, has_before2 = me + 2 <= last_seq, me >= 2
    odd = lax.rem(me, 2)
    up, down = me + 3 - 4 * odd, me + 1 - 4 * odd
    carries_up = (down >= 0) & (down + 2 <= last_seq)
    carries_down = (up <= last_seq) & (up >= 2)

    cut = CUT
    mid = CUT + (img - CUT + 16) // 32 * 16
    piece_a, piece_b = pl.ds(0, cut), pl.ds(cut, img - cut)
    halves = (pl.ds(cut, mid - cut), pl.ds(mid, img - mid))
    via_halves = (pl.ds(0, mid - cut), pl.ds(mid - cut, img - mid))

    def cols(g):
        return pl.ds(g * HD, HD)

    loads = []
    for g in range(kv):
        loads.append(pltpu.make_async_copy(keys.at[0, :, cols(g)], cand[g].at[0, 0], load_sem.at[2 * g]))
        loads.append(pltpu.make_async_copy(values.at[0, :, cols(g)], cand[g].at[0, 1], load_sem.at[2 * g + 1]))
    loads.append(pltpu.make_async_copy(query, q_in, load_sem.at[2 * kv]))
    loads.append(pltpu.make_async_copy(cotangent, g_in, load_sem.at[2 * kv + 1]))
    for load in loads:
        load.start()

    barrier = pltpu.get_barrier_semaphore()
    for there, index in (
        (has_before, before), (has_after, after),
        (carries_up, down), (has_before2, down),
        (carries_down, up), (has_after2, up),
    ):
        @pl.when(there)
        def _(index=index):
            pl.semaphore_signal(barrier, inc=1, device_id={"seq": index}, device_id_type=MESH)

    for step in range(1, n_head):
        pl.semaphore_signal(
            barrier, inc=1, device_id={"head": lax.rem(head + step, n_head)}, device_id_type=MESH
        )
    receivers = (has_after, has_before, has_after2, carries_up, has_before2, carries_down)
    count = n_head - 1
    for there in receivers:
        count = count + there.astype(jnp.int32)
    for load in loads[: 2 * kv]:
        load.wait()
    pl.semaphore_wait(barrier, count)

    def remote(source, target, sems, g, slot, index):
        return pltpu.make_async_remote_copy(
            source, target, sems[0].at[g, slot], sems[1].at[g, slot],
            device_id={"seq": index}, device_id_type=MESH,
        )

    def fwd(g, slot):
        near, distant = cand[g].at[1], cand[g].at[2]
        mine = cand[g].at[0]
        source, target, index = (
            (mine.at[:, piece_a], near.at[:, piece_a], after),
            (mine.at[:, halves[0]], via_f.at[g, :, via_halves[0]], up),
            (mine.at[:, piece_b], near.at[:, piece_b], after),
            (mine.at[:, halves[1]], via_f.at[g, :, via_halves[1]], up),
            (near.at[:, piece_a], distant.at[:, piece_a], after),
            (via_f.at[g, :, via_halves[0]], distant.at[:, halves[0]], up),
            (via_f.at[g, :, via_halves[1]], distant.at[:, halves[1]], up),
        )[slot]
        return remote(source, target, (fwd_send, fwd_recv), g, slot, index)

    fwd_starts = (has_after, has_after2, has_after, has_after2, has_before & has_after, carries_up, carries_up)
    fwd_comes = (has_before, carries_up, has_before, carries_up, has_before2, has_before2, has_before2)

    def bwd(g, slot):
        source, target, index = (
            (out2a.at[g], got2a.at[g], before),
            (out2b.at[g, :, via_halves[0]], via_b.at[g, :, via_halves[0]], down),
            (out2b.at[g, :, via_halves[1]], via_b.at[g, :, via_halves[1]], down),
            (out1b.at[g], got1b.at[g], before),
            (out1a.at[g], got1a.at[g], before),
            (via_b.at[g, :, via_halves[0]], far1b.at[g, :, via_halves[0]], down),
            (via_b.at[g, :, via_halves[1]], far1b.at[g, :, via_halves[1]], down),
        )[slot]
        return remote(source, target, (bwd_send, bwd_recv), g, slot, index)

    bwd_starts = (has_before2, has_before2, has_before2, has_before, has_before, carries_down, carries_down)
    bwd_comes = (
        has_before & has_after, carries_down, carries_down, has_after, has_after, has_after2, has_after2,
    )

    def start(kind, g, slot):
        @pl.when((fwd_starts if kind is fwd else bwd_starts)[slot])
        def _():
            kind(g, slot).start()

    def sent(kind, g, slot):
        @pl.when((fwd_starts if kind is fwd else bwd_starts)[slot])
        def _():
            kind(g, slot).wait_send()

    def come(kind, g, slot):
        @pl.when((fwd_comes if kind is fwd else bwd_comes)[slot])
        def _():
            kind(g, slot).wait_recv()

    def fwd_start(g):
        for slot in range(4):
            start(fwd, g, slot)

    def fwd_pass_on(g):
        for first, second in ((0, 4), (1, 5), (3, 6)):
            come(fwd, g, first)
            start(fwd, g, second)

    def fwd_arrive(g):
        for slot in (2, 4, 5, 6):
            come(fwd, g, slot)

    def bwd_add(g):
        come(bwd, g, 0)
        out1a[g] = (out1a[g].astype(F32) + got2a[g].astype(F32)).astype(BF16)
        start(bwd, g, 4)

    def bwd_pass_on(g, half):
        come(bwd, g, 1 + half)
        start(bwd, g, 5 + half)

    def bwd_arrive(g):
        for slot in range(3, 7):
            come(bwd, g, slot)

    def dq_place(g):
        return query_rows.at[:, pl.ds(pl.multiple_of(head * kv * width + g * width, HD), width)]

    def dq_copy(g, step, target):
        return pltpu.make_async_remote_copy(
            dq_out.at[g, step], dq_place(g), dq_send.at[g, step], dq_recv.at[g, step],
            device_id={"head": target}, device_id_type=MESH,
        )

    def dq_keep(g):
        return pltpu.make_async_copy(dq_out.at[g, blocks - 1], dq_place(g), dq_own.at[g])

    def att_store(g):
        columns = pl.ds(g * width, width)
        return pltpu.make_async_copy(att.at[:, columns], attended.at[:, columns], store_sem.at[2 * kv + g])

    def distance(j, b):
        return jnp.clip(me - owner_map[read_lists[j, b]], 0, 2)

    def block_at(step):
        pair, core = head // 2, lax.rem(head, 2)
        return lax.rem(pair + 1 - step // 2, 2) * 2 + lax.rem(core + (step + 1) // 2, 2)

    def rows_of(b):
        return pl.ds(pl.multiple_of(b * BLOCK, BLOCK), BLOCK)

    def at_head(g, h):
        return pl.ds((g * group + h) * HD, HD)

    def make_dq(g, step, b, k0, k1, c0, c1):
        dq = (dot(k0, c0, 0, 0) + dot(k1, c1, 0, 0)) * SCALE
        for h in range(group):
            dq_out[g, step, :, h * HD : (h + 1) * HD] = dq[:, h * HD : (h + 1) * HD].T.astype(BF16)

        @pl.when(step < blocks - 1)
        def _():
            dq_copy(g, step, b).start()

        @pl.when(step == blocks - 1)
        def _():
            dq_keep(g).start()

    def make_out(g, b, v0, v1, w0, w1):
        out = dot(v0, w0, 0, 0) + dot(v1, w1, 0, 0)
        for h in range(group):
            att[rows_of(b), at_head(g, h)] = out[:, h * HD : (h + 1) * HD].T.astype(BF16)

    def main_step(g, step, late):
        b = block_at(step)
        first, second = distance(0, b), distance(1, b)
        live0, live1 = visible[0, b] > 0, visible[1, b] > 0
        k0, k1 = cand[g][first, 0], cand[g][second, 0]
        v0, v1 = cand[g][first, 1], cand[g][second, 1]
        qc = jnp.concatenate([q_in[rows_of(b), at_head(g, h)] for h in range(group)], axis=0)
        gc = jnp.concatenate([g_in[rows_of(b), at_head(g, h)] for h in range(group)], axis=0)
        s0, s1 = dot(k0, qc, 1, 1), dot(k1, qc, 1, 1)
        m0 = jnp.max(s0, axis=0, keepdims=True)
        m1 = jnp.max(s1, axis=0, keepdims=True)
        m = jnp.maximum(jnp.where(live0, m0, -FAR), jnp.where(live1, m1, -FAR)) * TO_EXP2
        e0 = jnp.exp2(s0 * TO_EXP2 - jnp.where(live0, m, FAR))
        e1 = jnp.exp2(s1 * TO_EXP2 - jnp.where(live1, m, FAR))
        total = jnp.sum(e0, axis=0, keepdims=True) + jnp.sum(e1, axis=0, keepdims=True)
        inverse = jnp.where(live0 | live1, 1.0 / jnp.where(live0 | live1, total, 1.0), 0.0)
        p0, p1 = e0 * inverse, e1 * inverse
        w0, w1 = p0.astype(BF16), p1.astype(BF16)
        d0, d1 = dot(v0, gc, 1, 1), dot(v1, gc, 1, 1)
        row_dot = jnp.sum(p0 * d0, axis=0, keepdims=True) + jnp.sum(p1 * d1, axis=0, keepdims=True)
        c0 = (p0 * (d0 - row_dot)).astype(BF16)
        c1 = (p1 * (d1 - row_dot)).astype(BF16)
        make_dq(g, step, b, k0, k1, c0, c1)
        if late:
            soft[b, 0], soft[b, 1] = w0, w1
        else:
            make_out(g, b, v0, v1, w0, w1)
        parts[b, 0, 0] = dot(c0, qc, 1, 0) * SCALE
        parts[b, 0, 1] = dot(w0, gc, 1, 0)
        parts[b, 1, 0] = dot(c1, qc, 1, 0) * SCALE
        parts[b, 1, 1] = dot(w1, gc, 1, 0)

    fwd_start(0)

    @pl.when(me < 2)
    def _():
        for g in range(kv):
            cand[g][2] = jnp.zeros((2, img, HD), BF16)

    @pl.when(me < 1)
    def _():
        for g in range(kv):
            cand[g][1] = jnp.zeros((2, img, HD), BF16)

    @pl.when((me == 0) | (me == last_seq))
    def _():
        got2a[...] = jnp.zeros_like(got2a)

    @pl.when(me == last_seq)
    def _():
        got1a[...] = jnp.zeros_like(got1a)
        got1b[...] = jnp.zeros_like(got1b)

    @pl.when(me + 2 > last_seq)
    def _():
        far1b[...] = jnp.zeros_like(far1b)

    parts[:, 2] = jnp.zeros((blocks, 2, img, HD), F32)
    fwd_pass_on(0)
    for g in range(1, kv):
        fwd_start(g)
    for load in loads[2 * kv :]:
        load.wait()

    away = [[distance(j, b) for j in range(2)] for b in range(blocks)]

    def part_sum(slot, part, piece):
        total = None
        for b in range(blocks):
            pick = jnp.where(away[b][0] == slot, 0, jnp.where(away[b][1] == slot, 1, 2))
            both = (away[b][0] == slot) & (away[b][1] == slot) & (visible[1, b] > 0)
            term = parts[b, jnp.where(both, 1, pick), part, piece]
            total = term if total is None else total + term
        return total

    for g in range(kv):
        late = g == kv - 1
        fwd_arrive(g)

        def block_step(step, carry, g=g, late=late):
            main_step(g, step, late)

            @pl.when(step == 1)
            def _():
                if g + 1 < kv:
                    fwd_pass_on(g + 1)
                if g > 0:
                    bwd_add(g - 1)
                    bwd_pass_on(g - 1, 0)
                    bwd_pass_on(g - 1, 1)

            return carry

        lax.fori_loop(0, blocks, block_step, 0)
        for part in range(2):
            out2a[g, part] = part_sum(2, part, piece_a).astype(BF16)
        start(bwd, g, 0)
        for part in range(2):
            out2b[g, part] = part_sum(2, part, piece_b).astype(BF16)
        start(bwd, g, 1)
        start(bwd, g, 2)
        for part in range(2):
            out1b[g, part] = part_sum(1, part, piece_b).astype(BF16)
        start(bwd, g, 3)
        for part in range(2):
            out1a[g, part] = part_sum(1, part, piece_a).astype(BF16)
        for part in range(2):
            own[g, part] = part_sum(0, part, pl.ds(0, img))
        if not late:
            att_store(g).start()

    last = kv - 1

    def late_out(b, carry):
        v0, v1 = cand[last][distance(0, b), 1], cand[last][distance(1, b), 1]
        make_out(last, b, v0, v1, soft[b, 0], soft[b, 1])

        @pl.when(b == 1)
        def _():
            bwd_add(last)
            bwd_pass_on(last, 0)

        return carry

    lax.fori_loop(0, blocks, late_out, 0)
    bwd_pass_on(last, 1)
    att_store(last).start()

    stores = []
    for g in range(kv):
        bwd_arrive(g)
        for part, target in ((0, key_grad), (1, value_grad)):
            result[g, part, piece_a] = (own[g, part, piece_a] + got1a[g, part].astype(F32)).astype(BF16)
            result[g, part, piece_b] = (
                own[g, part, piece_b] + got1b[g, part].astype(F32) + far1b[g, part].astype(F32)
            ).astype(BF16)
            store = pltpu.make_async_copy(
                result.at[g, part], target.at[0, :, cols(g)], store_sem.at[2 * g + part]
            )
            store.start()
            stores.append(store)
    for g in range(kv):
        for step in range(blocks - 1):
            copy = dq_copy(g, step, head)
            copy.wait_send()
            copy.wait_recv()
        dq_keep(g).wait()
        att_store(g).wait()
        for slot in range(7):
            sent(fwd, g, slot)
            sent(bwd, g, slot)
    for store in stores:
        store.wait()


def hand_on(*refs):
    count = (len(refs) - 2) // 3
    sources, targets, holds = refs[:count], refs[count : 2 * count], refs[2 * count : 3 * count]
    sems = refs[3 * count :]
    ins, outs = [], []
    for i in range(count):
        rows = sources[i].shape[-2] // PIECES
        for piece in range(PIECES):
            at = (pl.ds(piece * rows, rows),) if len(sources[i].shape) == 2 else (0, pl.ds(piece * rows, rows))
            ins.append(pltpu.make_async_copy(sources[i].at[at], holds[i].at[at], sems[0].at[i, piece]))
            outs.append(pltpu.make_async_copy(holds[i].at[at], targets[i].at[at], sems[1].at[i, piece]))
    for copy in ins:
        copy.start()
    for first, second in zip(ins, outs):
        first.wait()
        second.start()
    for copy in outs:
        copy.wait()


def body(query, keys, values, cotangent, owner_map, read_lists, visible):
    rows, columns = query.shape
    img, kv_columns = keys.shape[1:]
    n_seq, n_head = lax.axis_size("seq"), lax.axis_size("head")
    kv = kv_columns // HD
    group = columns // kv_columns
    blocks = rows // BLOCK
    width = group * HD
    sizes = (n_seq, n_head, kv, group, blocks, img)
    any_space = pl.BlockSpec(memory_space=pl.ANY)
    scalar = pl.BlockSpec(memory_space=pltpu.SMEM)
    dma = pltpu.SemaphoreType.DMA
    low, high = CUT, img - CUT
    outs = (
        jax.ShapeDtypeStruct((rows, columns), BF16),
        jax.ShapeDtypeStruct((rows // n_head, columns * n_head), BF16),
        jax.ShapeDtypeStruct(keys.shape, BF16),
        jax.ShapeDtypeStruct(values.shape, BF16),
    )
    made = pl.pallas_call(
        functools.partial(kernel, sizes),
        out_shape=outs,
        in_specs=[any_space] * 4 + [scalar] * 3,
        out_specs=(any_space,) * 4,
        scratch_shapes=[
            pltpu.VMEM((rows, columns), BF16),
            pltpu.VMEM((rows, columns), BF16),
            tuple(pltpu.VMEM((3, 2, img, HD), BF16) for _ in range(kv)),
            pltpu.VMEM((kv, 2, high, HD), BF16),
            pltpu.VMEM((rows, columns), BF16),
            pltpu.VMEM((kv, blocks, BLOCK, width), BF16),
            pltpu.VMEM((blocks, 2, img, width), BF16),
            pltpu.VMEM((blocks, 3, 2, img, HD), F32),
            pltpu.VMEM((kv, 2, low, HD), BF16),
            pltpu.VMEM((kv, 2, high, HD), BF16),
            pltpu.VMEM((kv, 2, low, HD), BF16),
            pltpu.VMEM((kv, 2, high, HD), BF16),
            pltpu.VMEM((kv, 2, low, HD), BF16),
            pltpu.VMEM((kv, 2, low, HD), BF16),
            pltpu.VMEM((kv, 2, high, HD), BF16),
            pltpu.VMEM((kv, 2, high, HD), BF16),
            pltpu.VMEM((kv, 2, high, HD), BF16),
            pltpu.VMEM((kv, 2, img, HD), F32),
            pltpu.VMEM((kv, 2, img, HD), BF16),
            dma((2 * kv + 2,)),
            dma((3 * kv,)),
            dma((kv, 7)),
            dma((kv, 7)),
            dma((kv, 7)),
            dma((kv, 7)),
            dma((kv, blocks)),
            dma((kv, blocks)),
            dma((kv,)),
        ],
        compiler_params=pltpu.CompilerParams(
            collective_id=0, has_side_effects=True, vmem_limit_bytes=56 * 2**20
        ),
        name="cross_attention",
    )(query, keys, values, cotangent, owner_map, read_lists.T, visible.T)
    return pl.pallas_call(
        hand_on,
        out_shape=outs,
        in_specs=[any_space] * 4,
        out_specs=(any_space,) * 4,
        scratch_shapes=[pltpu.VMEM(o.shape, o.dtype) for o in outs] + [dma((4, PIECES))] * 2,
        compiler_params=pltpu.CompilerParams(vmem_limit_bytes=56 * 2**20),
        name="hand_on",
    )(*made)


def solution(mesh):
    in_specs = (
        P("seq", "head"),
        P("seq", None, "head"),
        P("seq", None, "head"),
        P("seq", "head"),
        P(),
        P("seq", None),
        P("seq", None),
    )
    out_specs = (
        P("seq", "head"),
        P(("seq", "head"), None),
        P("seq", None, "head"),
        P("seq", None, "head"),
    )
    return jax.shard_map(body, mesh=mesh, in_specs=in_specs, out_specs=out_specs, check_vma=False)
```

```python
import functools
import math

import jax
import jax.numpy as jnp
from jax import lax
from jax.experimental import pallas as pl
from jax.experimental.pallas import tpu as pltpu
from jax.sharding import PartitionSpec as P

HD = 128
BLOCK = 128
MESH = pl.DeviceIdType.MESH
F32, BF16 = jnp.float32, jnp.bfloat16
SCALE = 1.0 / math.sqrt(HD)
TO_EXP2 = SCALE * math.log2(math.e)
FAR = 1e30
CUT = 176
PIECES = 4


def dot(a, b, ca, cb):
    return lax.dot_general(a, b, (((ca,), (cb,)), ((), ())), preferred_element_type=F32)


def kernel(
    sizes,
    query, keys, values, cotangent, owner_map, read_lists, visible,
    attended, query_rows, key_grad, value_grad,
    q_in, g_in, cand, via_f, dq_out, soft, dsc, invs, wide, parts,
    out2a, out2b, out1a, out1b, got2a, got1a, got1b, via_b, far1b, own,
    load_sem, fwd_send, fwd_recv, bwd_send, bwd_recv, dq_send, dq_recv, dq_own,
):
    n_seq, n_head, kv, group, blocks, img = sizes
    me = lax.axis_index("seq")
    head = lax.axis_index("head")
    width = group * HD

    last_seq = n_seq - 1
    after, before = me + 1, me - 1
    has_after, has_before = me < last_seq, me > 0
    has_after2, has_before2 = me + 2 <= last_seq, me >= 2
    odd = lax.rem(me, 2)
    up, down = me + 3 - 4 * odd, me + 1 - 4 * odd
    carries_up = (down >= 0) & (down + 2 <= last_seq)
    carries_down = (up <= last_seq) & (up >= 2)

    cut = CUT
    mid = CUT + (img - CUT + 16) // 32 * 16
    piece_a, piece_b = pl.ds(0, cut), pl.ds(cut, img - cut)
    halves = (pl.ds(cut, mid - cut), pl.ds(mid, img - mid))
    via_halves = (pl.ds(0, mid - cut), pl.ds(mid - cut, img - mid))

    def cols(g):
        return pl.ds(g * HD, HD)

    loads = []
    for g in range(kv):
        for part, source in ((0, keys), (1, values)):
            sem = load_sem.at[2 * g + part]
            loads.append(pltpu.make_async_copy(source.at[0, :, cols(g)], cand[g][part].at[0], sem))
    loads.append(pltpu.make_async_copy(query, q_in, load_sem.at[2 * kv]))
    loads.append(pltpu.make_async_copy(cotangent, g_in, load_sem.at[2 * kv + 1]))
    for load in loads:
        load.start()

    barrier = pltpu.get_barrier_semaphore()
    for there, index in (
        (has_before, before), (has_after, after),
        (carries_up, down), (has_before2, down),
        (carries_down, up), (has_after2, up),
    ):
        @pl.when(there)
        def _(index=index):
            pl.semaphore_signal(barrier, inc=1, device_id={"seq": index}, device_id_type=MESH)

    for step in range(1, n_head):
        pl.semaphore_signal(
            barrier, inc=1, device_id={"head": lax.rem(head + step, n_head)}, device_id_type=MESH
        )
    receivers = (has_after, has_before, has_after2, carries_up, has_before2, carries_down)
    count = n_head - 1
    for there in receivers:
        count = count + there.astype(jnp.int32)
    for load in loads[: 2 * kv]:
        load.wait()
    pl.semaphore_wait(barrier, count)

    def remote(source, target, sems, stage, slot, index):
        return pltpu.make_async_remote_copy(
            source, target, sems[0].at[stage, slot], sems[1].at[stage, slot],
            device_id={"seq": index}, device_id_type=MESH,
        )

    def fwd(stage, slot):
        here, via = cand[stage // 2][stage % 2], via_f.at[stage]
        mine, near, distant = here.at[0], here.at[1], here.at[2]
        source, target, index = (
            (mine.at[piece_a], near.at[piece_a], after),
            (mine.at[halves[0]], via.at[via_halves[0]], up),
            (mine.at[piece_b], near.at[piece_b], after),
            (mine.at[halves[1]], via.at[via_halves[1]], up),
            (near.at[piece_a], distant.at[piece_a], after),
            (via.at[via_halves[0]], distant.at[halves[0]], up),
            (via.at[via_halves[1]], distant.at[halves[1]], up),
        )[slot]
        return remote(source, target, (fwd_send, fwd_recv), stage, slot, index)

    def bwd(stage, slot):
        source, target, index = (
            (out2a.at[stage], got2a.at[stage], before),
            (out2b.at[stage, via_halves[0]], via_b.at[stage, via_halves[0]], down),
            (out2b.at[stage, via_halves[1]], via_b.at[stage, via_halves[1]], down),
            (out1b.at[stage], got1b.at[stage], before),
            (out1a.at[stage], got1a.at[stage], before),
            (via_b.at[stage, via_halves[0]], far1b.at[stage, via_halves[0]], down),
            (via_b.at[stage, via_halves[1]], far1b.at[stage, via_halves[1]], down),
        )[slot]
        return remote(source, target, (bwd_send, bwd_recv), stage, slot, index)

    fwd_starts = (has_after, has_after2, has_after, has_after2, has_before & has_after, carries_up, carries_up)
    fwd_comes = (has_before, carries_up, has_before, carries_up, has_before2, has_before2, has_before2)

    bwd_starts = (has_before2, has_before2, has_before2, has_before, has_before, carries_down, carries_down)
    bwd_comes = (
        has_before & has_after, carries_down, carries_down, has_after, has_after, has_after2, has_after2,
    )

    def start(kind, g, slot):
        @pl.when((fwd_starts if kind is fwd else bwd_starts)[slot])
        def _():
            kind(g, slot).start()

    def sent(kind, g, slot):
        @pl.when((fwd_starts if kind is fwd else bwd_starts)[slot])
        def _():
            kind(g, slot).wait_send()

    def come(kind, g, slot):
        @pl.when((fwd_comes if kind is fwd else bwd_comes)[slot])
        def _():
            kind(g, slot).wait_recv()

    def fwd_start(g):
        for slot in range(4):
            start(fwd, g, slot)

    def fwd_pass_on(g):
        for first, second in ((0, 4), (1, 5), (3, 6)):
            come(fwd, g, first)
            start(fwd, g, second)

    def fwd_arrive(g):
        for slot in (2, 4, 5, 6):
            come(fwd, g, slot)

    def bwd_add(g):
        come(bwd, g, 0)
        out1a[g] = (out1a[g].astype(F32) + got2a[g].astype(F32)).astype(BF16)
        start(bwd, g, 4)

    def bwd_pass_on(g):
        for half in range(2):
            come(bwd, g, 1 + half)
            start(bwd, g, 5 + half)

    def bwd_arrive(g):
        for slot in range(3, 7):
            come(bwd, g, slot)

    def dq_place(g):
        return query_rows.at[:, pl.ds(pl.multiple_of(head * kv * width + g * width, HD), width)]

    def dq_copy(g, step, target):
        return pltpu.make_async_remote_copy(
            dq_out.at[g, step], dq_place(g), dq_send.at[g, step], dq_recv.at[g, step],
            device_id={"head": target}, device_id_type=MESH,
        )

    def dq_keep(g):
        return pltpu.make_async_copy(dq_out.at[g, blocks - 1], dq_place(g), dq_own.at[g])

    def distance(j, b):
        return jnp.clip(me - owner_map[read_lists[j, b]], 0, 2)

    def block_at(step):
        pair, core = head // 2, lax.rem(head, 2)
        return lax.rem(pair + 1 - step // 2, 2) * 2 + lax.rem(core + (step + 1) // 2, 2)

    def rows_of(b):
        return pl.ds(pl.multiple_of(b * BLOCK, BLOCK), BLOCK)

    def at_head(g, h):
        return pl.ds((g * group + h) * HD, HD)

    def rows_at(ref, g, b):
        return jnp.concatenate([ref[rows_of(b), at_head(g, h)] for h in range(group)], axis=0)

    def pair_of(g, part, b):
        return cand[g][part][distance(0, b)], cand[g][part][distance(1, b)]

    def scores(g, b):
        k0, k1 = pair_of(g, 0, b)
        rows = rows_at(q_in, g, b)
        return dot(k0, rows, 1, 1), dot(k1, rows, 1, 1)

    def weigh(g, b, s0, s1):
        live0, live1 = visible[0, b] > 0, visible[1, b] > 0
        m0 = jnp.max(s0, axis=0, keepdims=True)
        m1 = jnp.max(s1, axis=0, keepdims=True)
        m = jnp.maximum(jnp.where(live0, m0, -FAR), jnp.where(live1, m1, -FAR)) * TO_EXP2
        e0 = jnp.exp2(s0 * TO_EXP2 - jnp.where(live0, m, FAR))
        e1 = jnp.exp2(s1 * TO_EXP2 - jnp.where(live1, m, FAR))
        total = jnp.sum(e0, axis=0, keepdims=True) + jnp.sum(e1, axis=0, keepdims=True)
        soft[b, 0], soft[b, 1] = e0.astype(BF16), e1.astype(BF16)
        inverse = jnp.where(live0 | live1, 1.0 / jnp.where(live0 | live1, total, 1.0), 0.0)
        column = jnp.broadcast_to(inverse, (8, width)).T[:, :1]
        invs[b] = column
        wide[b, :, :HD] = (rows_at(g_in, g, b).astype(F32) * column).astype(BF16)

    def make_out(g, b):
        v0, v1 = pair_of(g, 1, b)
        out = dot(v0, soft[b, 0], 0, 0) + dot(v1, soft[b, 1], 0, 0)
        lane = lax.broadcasted_iota(jnp.int32, (BLOCK, HD), 1)
        for h in range(group):
            rows = slice(h * HD, (h + 1) * HD)
            column = invs[b, rows]
            rounded = (out[:, rows].T * column).astype(BF16)
            attended[rows_of(b), at_head(g, h)] = rounded
            grad = g_in[rows_of(b), at_head(g, h)].astype(F32)
            row_dot = -jnp.sum(grad * rounded.astype(F32), axis=1, keepdims=True) * column
            high = row_dot.astype(BF16).astype(F32)
            both = jnp.where(lane == 0, high, jnp.where(lane == 1, row_dot - high, 0.0))
            wide[b, rows, HD:] = both.astype(BF16)

    def dprob_less_dot(g, b):
        lane = lax.broadcasted_iota(jnp.int32, (img, HD), 1)
        ones = jnp.where(lane < 2, 1.0, 0.0).astype(BF16)
        rows = wide[b]
        return tuple(dot(jnp.concatenate([v, ones], axis=1), rows, 1, 1) for v in pair_of(g, 1, b))

    def dscores(b, d0, d1):
        dsc[b, 0] = (soft[b, 0].astype(F32) * d0).astype(BF16)
        dsc[b, 1] = (soft[b, 1].astype(F32) * d1).astype(BF16)

    def value_part(b):
        rows = wide[b, :, :HD]
        for j in range(2):
            parts[b, j, 1] = dot(soft[b, j], rows, 1, 0)

    def key_part(g, b):
        rows = rows_at(q_in, g, b)
        for j in range(2):
            parts[b, j, 0] = dot(dsc[b, j], rows, 1, 0)

    def make_dq(g, step, b):
        k0, k1 = pair_of(g, 0, b)
        dq = (dot(k0, dsc[b, 0], 0, 0) + dot(k1, dsc[b, 1], 0, 0)) * SCALE
        for h in range(group):
            dq_out[g, step, :, h * HD : (h + 1) * HD] = dq[:, h * HD : (h + 1) * HD].T.astype(BF16)

    def send_dq(g, step, b):
        @pl.when(step < blocks - 1)
        def _():
            dq_copy(g, step, b).start()

        @pl.when(step == blocks - 1)
        def _():
            dq_keep(g).start()

    def pair_at(i):
        return block_at(2 * i), block_at(2 * i + 1)

    def finish_pair(g, i, p, with_dq):
        b, c = pair_at(i)
        dscores(b, *p)
        r = dprob_less_dot(g, c)
        key_part(g, b)
        if with_dq:
            make_dq(g, 2 * i, b)
        dscores(c, *r)
        key_part(g, c)
        if with_dq:
            make_dq(g, 2 * i + 1, c)
            send_dq(g, 2 * i, b)
            send_dq(g, 2 * i + 1, c)

    def whole_pair(g, i, with_dq):
        b, c = pair_at(i)
        s, t = scores(g, b), scores(g, c)
        weigh(g, b, *s)
        make_out(g, b)
        value_part(b)
        weigh(g, c, *t)
        p = dprob_less_dot(g, b)
        make_out(g, c)
        value_part(c)
        finish_pair(g, i, p, with_dq)

    def pair_weights(g, i):
        b, c = pair_at(i)
        s, t = scores(g, b), scores(g, c)
        weigh(g, b, *s)
        weigh(g, c, *t)

    def pair_after_weights(g, i, with_dq):
        b, c = pair_at(i)
        make_out(g, b)
        value_part(b)
        make_out(g, c)
        p = dprob_less_dot(g, b)
        value_part(c)
        finish_pair(g, i, p, with_dq)

    def pair_to_values(g, i):
        b, c = pair_at(i)
        s, t = scores(g, b), scores(g, c)
        weigh(g, b, *s)
        make_out(g, b)
        value_part(b)
        weigh(g, c, *t)
        make_out(g, c)
        value_part(c)

    def pair_after_values(g, i, with_dq):
        b, c = pair_at(i)
        finish_pair(g, i, dprob_less_dot(g, b), with_dq)

    fwd_start(0)

    @pl.when(me < 2)
    def _():
        for g in range(kv):
            for part in range(2):
                cand[g][part][2] = jnp.zeros((img, HD), BF16)

    @pl.when(me < 1)
    def _():
        for g in range(kv):
            for part in range(2):
                cand[g][part][1] = jnp.zeros((img, HD), BF16)

    @pl.when((me == 0) | (me == last_seq))
    def _():
        got2a[...] = jnp.zeros_like(got2a)

    @pl.when(me == last_seq)
    def _():
        got1a[...] = jnp.zeros_like(got1a)
        got1b[...] = jnp.zeros_like(got1b)

    @pl.when(me + 2 > last_seq)
    def _():
        far1b[...] = jnp.zeros_like(far1b)

    parts[:, 2] = jnp.zeros((blocks, 2, img, HD), F32)
    fwd_pass_on(0)
    fwd_start(1)
    for load in loads[2 * kv :]:
        load.wait()

    away = [[distance(j, b) for j in range(2)] for b in range(blocks)]

    def part_sum(slot, part, piece):
        total = None
        for b in range(blocks):
            pick = jnp.where(away[b][0] == slot, 0, jnp.where(away[b][1] == slot, 1, 2))
            both = (away[b][0] == slot) & (away[b][1] == slot) & (visible[1, b] > 0)
            term = parts[b, jnp.where(both, 1, pick), part, piece]
            total = term if total is None else total + term
        return total

    def send_parts(g, part):
        stage = 2 * g + part
        factor = 1.0 if part else SCALE
        out2a[stage] = (part_sum(2, part, piece_a) * factor).astype(BF16)
        start(bwd, stage, 0)
        out2b[stage] = (part_sum(2, part, piece_b) * factor).astype(BF16)
        start(bwd, stage, 1)
        start(bwd, stage, 2)
        out1b[stage] = (part_sum(1, part, piece_b) * factor).astype(BF16)
        start(bwd, stage, 3)
        out1a[stage] = (part_sum(1, part, piece_a) * factor).astype(BF16)
        own[stage] = part_sum(0, part, pl.ds(0, img)) * factor

    def finish(g, part):
        stage = 2 * g + part
        target = value_grad if part else key_grad
        bwd_arrive(stage)
        target[0, piece_a, cols(g)] = (own[stage, piece_a] + got1a[stage].astype(F32)).astype(BF16)
        target[0, piece_b, cols(g)] = (
            own[stage, piece_b] + got1b[stage].astype(F32) + far1b[stage].astype(F32)
        ).astype(BF16)

    def handle(stage):
        bwd_add(stage)
        bwd_pass_on(stage)

    last = kv - 1
    pairs = blocks // 2
    for g in range(kv):
        fwd_arrive(2 * g)
        if g == 0:
            fwd_pass_on(1)
            for stage in range(2, 2 * kv):
                fwd_start(stage)
            pair_weights(g, 0)
        fwd_arrive(2 * g + 1)
        if g == 0:
            pair_after_weights(g, 0, True)
        else:
            whole_pair(g, 0, True)
        if g < last:
            fwd_pass_on(2 * g + 2)
            fwd_pass_on(2 * g + 3)
        if g > 0:
            handle(2 * g - 1)
            handle(2 * g - 2)
        for i in range(1, pairs):
            if g == last and i == pairs - 1:
                pair_to_values(g, i)
                send_parts(g, 1)
                pair_after_values(g, i, False)
            else:
                whole_pair(g, i, True)
        if g < last:
            send_parts(g, 1)
        send_parts(g, 0)
    handle(2 * last + 1)
    for step in range(blocks - 2, blocks):
        make_dq(last, step, block_at(step))
        send_dq(last, step, block_at(step))
    handle(2 * last)

    for g in range(kv):
        finish(g, 1)
        finish(g, 0)
    for g in range(kv):
        for step in range(blocks - 1):
            copy = dq_copy(g, step, head)
            copy.wait_send()
            copy.wait_recv()
        dq_keep(g).wait()
        for part in range(2):
            for slot in range(7):
                sent(fwd, 2 * g + part, slot)
                sent(bwd, 2 * g + part, slot)


def hand_on(*refs):
    count = (len(refs) - 1) // 2
    sources, targets, sems = refs[:count], refs[count : 2 * count], refs[-1]
    copies = []
    for i in range(count):
        rows = sources[i].shape[-2] // PIECES
        for piece in range(PIECES):
            at = (pl.ds(piece * rows, rows),) if len(sources[i].shape) == 2 else (0, pl.ds(piece * rows, rows))
            copies.append(pltpu.make_async_copy(sources[i].at[at], targets[i].at[at], sems.at[i, piece]))
    for copy in copies:
        copy.start()
    for copy in copies:
        copy.wait()


def body(query, keys, values, cotangent, owner_map, read_lists, visible):
    rows, columns = query.shape
    img, kv_columns = keys.shape[1:]
    n_seq, n_head = lax.axis_size("seq"), lax.axis_size("head")
    kv = kv_columns // HD
    group = columns // kv_columns
    blocks = rows // BLOCK
    width = group * HD
    sizes = (n_seq, n_head, kv, group, blocks, img)
    any_space = pl.BlockSpec(memory_space=pl.ANY)
    scalar = pl.BlockSpec(memory_space=pltpu.SMEM)
    dma = pltpu.SemaphoreType.DMA
    low, high = CUT, img - CUT
    outs = (
        jax.ShapeDtypeStruct((rows, columns), BF16),
        jax.ShapeDtypeStruct((rows // n_head, columns * n_head), BF16),
        jax.ShapeDtypeStruct(keys.shape, BF16),
        jax.ShapeDtypeStruct(values.shape, BF16),
    )
    made = pl.pallas_call(
        functools.partial(kernel, sizes),
        out_shape=tuple(pltpu.VMEM(o.shape, o.dtype) for o in outs),
        in_specs=[any_space] * 4 + [scalar] * 3,
        out_specs=(pl.BlockSpec(memory_space=pltpu.VMEM),) * 4,
        scratch_shapes=[
            pltpu.VMEM((rows, columns), BF16),
            pltpu.VMEM((rows, columns), BF16),
            tuple(tuple(pltpu.VMEM((3, img, HD), BF16) for _ in range(2)) for _ in range(kv)),
            pltpu.VMEM((2 * kv, high, HD), BF16),
            pltpu.VMEM((kv, blocks, BLOCK, width), BF16),
            pltpu.VMEM((blocks, 2, img, width), BF16),
            pltpu.VMEM((blocks, 2, img, width), BF16),
            pltpu.VMEM((blocks, width, 1), F32),
            pltpu.VMEM((blocks, width, 2 * HD), BF16),
            pltpu.VMEM((blocks, 3, 2, img, HD), F32),
            pltpu.VMEM((2 * kv, low, HD), BF16),
            pltpu.VMEM((2 * kv, high, HD), BF16),
            pltpu.VMEM((2 * kv, low, HD), BF16),
            pltpu.VMEM((2 * kv, high, HD), BF16),
            pltpu.VMEM((2 * kv, low, HD), BF16),
            pltpu.VMEM((2 * kv, low, HD), BF16),
            pltpu.VMEM((2 * kv, high, HD), BF16),
            pltpu.VMEM((2 * kv, high, HD), BF16),
            pltpu.VMEM((2 * kv, high, HD), BF16),
            pltpu.VMEM((2 * kv, img, HD), F32),
            dma((2 * kv + 2,)),
            dma((2 * kv, 7)),
            dma((2 * kv, 7)),
            dma((2 * kv, 7)),
            dma((2 * kv, 7)),
            dma((kv, blocks)),
            dma((kv, blocks)),
            dma((kv,)),
        ],
        compiler_params=pltpu.CompilerParams(
            collective_id=0, has_side_effects=True, vmem_limit_bytes=57 * 2**20
        ),
        name="cross_attention",
    )(query, keys, values, cotangent, owner_map, read_lists.T, visible.T)
    return pl.pallas_call(
        hand_on,
        out_shape=outs,
        in_specs=[pl.BlockSpec(memory_space=pltpu.VMEM)] * 4,
        out_specs=(any_space,) * 4,
        scratch_shapes=[dma((4, PIECES))],
        compiler_params=pltpu.CompilerParams(vmem_limit_bytes=4 * 2**20),
        name="hand_on",
    )(*(pltpu.with_memory_space_constraint(value, pltpu.VMEM) for value in made))


def solution(mesh):
    in_specs = (
        P("seq", "head"),
        P("seq", None, "head"),
        P("seq", None, "head"),
        P("seq", "head"),
        P(),
        P("seq", None),
        P("seq", None),
    )
    out_specs = (
        P("seq", "head"),
        P(("seq", "head"), None),
        P("seq", None, "head"),
        P("seq", None, "head"),
    )
    return jax.shard_map(body, mesh=mesh, in_specs=in_specs, out_specs=out_specs, check_vma=False)
```
